1024 devices in a mesh: section: 8 (over y), expert: 16 (over x, core), tensor: 8 (over z).
Axes of the slice: x: 8, y: 8, z: 8, core: 2. Of those that a mesh axis runs over, the one named last changes fastest.
Arguments:
- tokens: bfloat16 [16384, 4096], P(('section', 'expert'), 'tensor'), may hold values from -6 to 6
- w_gate: bfloat16 [8, 16, 4096, 1536], P('section', 'expert', None, 'tensor'), may hold values from -0.09375 to 0.09375
- w_up: bfloat16 [8, 16, 4096, 1536], P('section', 'expert', None, 'tensor'), may hold values from -0.09375 to 0.09375
- hidden_grad: bfloat16 [8, 16, 256, 1536], P('section', 'expert', None, 'tensor'), may hold values from -6 to 6
- routes: int32 [16384, 8], P(('section', 'expert')), may hold values from 0 to 127, as said below
- slots: int32 [16384, 8], P(('section', 'expert')), may hold values from 0 to 16, as said below
- pad_mask: int32 [16384], P(('section', 'expert')), may hold values 0 or 1
Outputs:
- upstream: bfloat16 [16384, 4096], P(('section', 'expert'), 'tensor')
The draws below stay inside these ranges and needn't reach their ends.
Inputs may be any that keep to these rules, and one draw needn't show every extreme that they name: `routes`: each row names 8 different experts. In every section one expert e with e mod 8 = 0 is named by 16 or more rows of every block of 128 rows. `slots`: within each block of 128 rows (the rows of one device), the routes naming one expert, taken in order of row and then of position in the row, hold 0, 1, 2 and so on; those from the 16-th on hold 16.
All inputs are finite; a program needn't handle non-finite values. No bound on the sum of `pad_mask` on one device may be relied on, other than what follows from the above.
Results may differ from the reference program's by a relative error of at most 0.018.
Values may be sent and summed in bfloat16 or wider, within the bound.
A program may use at most 32 MiB of HBM per device.

```python
import jax
import jax.numpy as jnp
from jax import lax

D = 4096
FF = 1536
TOPK = 8
EXP_DEV = 8
TOK_DEV = 128
EXPERTS = 128
CAP = 16
SLOTS = 256
TOKENS = 16384
N_SECTION = 8
N_EXPERT = 16
N_TENSOR = 8


def route_tables(key):
    blocks = TOKENS // TOK_DEV
    score_key, hot_key, bias_key = jax.random.split(key, 3)
    scores = jax.random.randint(score_key, (TOKENS, EXPERTS), 0, 1 << 16)
    bias = jax.random.randint(bias_key, (EXPERTS,), 0, 1 << 15)
    hot = EXP_DEV * jax.random.randint(hot_key, (N_SECTION,), 0, EXPERTS // EXP_DEV)
    row_ids = jnp.arange(TOKENS, dtype=jnp.int32)
    hot_row = jnp.take(hot, row_ids // (TOK_DEV * N_EXPERT))
    forced = row_ids % TOK_DEV % (TOK_DEV // CAP) == 0
    expert_ids = jnp.arange(EXPERTS, dtype=jnp.int32)
    total = (scores + bias[None, :]) * EXPERTS + expert_ids[None, :]
    total = total + jnp.where(forced[:, None] & (expert_ids[None, :] == hot_row[:, None]), 1 << 28, 0)
    _, chosen = lax.top_k(total, TOPK)
    chosen = chosen.astype(jnp.int32)
    onehot = (chosen[:, :, None] == expert_ids[None, None, :]).astype(jnp.int32)
    onehot = onehot.reshape(blocks, TOK_DEV * TOPK, EXPERTS)
    before = jnp.cumsum(onehot, axis=1) - onehot
    placed = jnp.sum(before * onehot, axis=2).reshape(TOKENS, TOPK)
    placed = jnp.minimum(placed, CAP).astype(jnp.int32)
    return (chosen, placed)


def draw_routes(key, part):
    chosen, placed = route_tables(key)
    return chosen


def draw_slots(key, part):
    chosen, placed = route_tables(key)
    return placed


def set_ends(values, own_key, low, top_value):
    dims = values.shape
    spot = [jax.random.randint(jax.random.fold_in(own_key, axis), (), 0, dims[axis]) for axis in range(len(dims))]
    values = values.at[tuple(spot)].set(low)
    longest = dims.index(max(dims))
    spot[longest] = (spot[longest] + 1) % dims[longest]
    return values.at[tuple(spot)].set(top_value)


def steps_of(key, extent, cuts, least, high):
    gain, own = 1.0, jax.random.fold_in(key, 6)
    for axis_at, parts in cuts:
        heights = jnp.exp(jax.random.uniform(jax.random.fold_in(own, axis_at), (parts,), jnp.float32, least / len(cuts), high / len(cuts)))
        gain = gain * jnp.repeat(heights, extent[axis_at] // parts).reshape([-1 if axis == axis_at else 1 for axis in range(len(extent))])
    return gain


def gaussian(own_key, dims, deviation, bound, shards=(), kind=jnp.bfloat16):
    factor_of = steps_of(own_key, dims, shards, -0.22, 0.18) if shards else 1.0
    array = jax.random.normal(own_key, dims, jnp.float32) * deviation * factor_of
    return jnp.minimum(jnp.maximum(array, -bound), bound).astype(kind)


def setup_inputs(seed: int = 0) -> dict:
    key_list = jax.random.split(jax.random.key(seed), 8)
    return {
        "tokens": gaussian(key_list[0], (TOKENS, D), 1.0, 6.0, ((0, 128), (1, 8))),
        "w_gate": gaussian(key_list[1], (N_SECTION, N_EXPERT, D, FF), D ** -0.5, 0.09375, ((0, 8), (1, 16), (3, 8))),
        "w_up": gaussian(key_list[2], (N_SECTION, N_EXPERT, D, FF), D ** -0.5, 0.09375, ((0, 8), (1, 16), (3, 8))),
        "hidden_grad": gaussian(key_list[3], (N_SECTION, N_EXPERT, SLOTS, FF), 1.0, 6.0, ((0, 8), (1, 16), (3, 8))),
        "routes": draw_routes(jax.random.fold_in(key_list[7], 71), 0),
        "slots": draw_slots(jax.random.fold_in(key_list[7], 71), 0),
        "pad_mask": set_ends((jax.random.randint(key_list[6], (TOKENS,), 0, 8) < 7).astype(jnp.int32), jax.random.fold_in(key_list[6], 1), 0, 1),
    }


def slot_table(routes, slots):
    live = (routes % EXP_DEV == 0) & (slots < CAP)
    target = jnp.where(live, routes // EXP_DEV * CAP + slots, -1).astype(jnp.int32)
    positions = lax.broadcasted_iota(jnp.int32, (SLOTS, routes.shape[0]), 0)
    hits = jnp.zeros((SLOTS, routes.shape[0]), jnp.float32)
    for k in range(routes.shape[1]):
        hits = hits + (positions == target[:, k][None, :]).astype(jnp.float32)
    return hits

def expert_grad(operands):
    x_rows, gate_w, up_w, grad_a = operands
    pre_gate = jnp.dot(x_rows, gate_w, preferred_element_type=jnp.float32)
    pre_up = jnp.dot(x_rows, up_w, preferred_element_type=jnp.float32)
    sig = jax.nn.sigmoid(pre_gate)
    act = grad_a.astype(jnp.float32)
    up_grad = (act * pre_gate * sig).astype(jnp.bfloat16)
    gate_grad = (act * pre_up * sig * (1.0 + pre_gate * (1.0 - sig))).astype(jnp.bfloat16)
    width = FF // N_TENSOR
    total = jnp.zeros((SLOTS, D), jnp.float32)
    for block in range(N_TENSOR):
        low = block * width
        term = lax.dot_general(gate_grad[:, low:low + width], gate_w[:, low:low + width], (((1,), (1,)), ((), ())), preferred_element_type=jnp.float32)
        term = term + lax.dot_general(up_grad[:, low:low + width], up_w[:, low:low + width], (((1,), (1,)), ((), ())), preferred_element_type=jnp.float32)
        rounded = lax.optimization_barrier(term.astype(jnp.bfloat16))
        total = total + rounded.astype(jnp.float32)
    return total

def reference(tokens, w_gate, w_up, hidden_grad, routes, slots, pad_mask):
    per_section = N_EXPERT * TOK_DEV
    results = []
    for section_index in range(N_SECTION):
        first = section_index * per_section
        x_section = tokens[first:first + per_section].reshape(N_EXPERT, TOK_DEV, D)
        r_section = routes[first:first + per_section].reshape(N_EXPERT, TOK_DEV, TOPK)
        s_section = slots[first:first + per_section].reshape(N_EXPERT, TOK_DEV, TOPK)
        m_section = pad_mask[first:first + per_section].reshape(N_EXPERT, TOK_DEV)
        hits = jax.vmap(slot_table)(r_section, s_section)
        sent = jnp.einsum('psn,pnd->psd', hits, x_section.astype(jnp.float32), precision=lax.Precision.HIGHEST)
        sent = sent.astype(jnp.bfloat16).reshape(N_EXPERT, N_EXPERT, CAP, D)
        arrived = jnp.transpose(sent, (1, 0, 2, 3)).reshape(N_EXPERT, SLOTS, D)
        slot_grad = lax.map(expert_grad, (arrived, w_gate[section_index], w_up[section_index], hidden_grad[section_index]))
        back = jnp.transpose(slot_grad.reshape(N_EXPERT, N_EXPERT, CAP, D), (1, 0, 2, 3)).reshape(N_EXPERT, SLOTS, D)
        keep = hits * m_section[:, None, :].astype(jnp.float32)
        grads = jnp.einsum('psn,psd->pnd', keep, back, precision=lax.Precision.HIGHEST)
        results.append(grads.reshape(per_section, D).astype(jnp.bfloat16))
    results = results[1:] + [jnp.zeros((per_section, D), jnp.bfloat16)]
    return jnp.concatenate(results, axis=0)
```

```python
import jax
import jax.numpy as jnp
from jax import lax
from jax.experimental import pallas as pl
from jax.experimental.pallas import tpu as pltpu
from jax.sharding import PartitionSpec as P

MESH = pl.DeviceIdType.MESH
EXP_DEV = 8
CAP = 16
ROUND = 8
CHIP = 2 * CAP
NEAR = (0, 1, 7, 2, 6, 3, 5, 4)
PLACE = tuple(NEAR.index(offset) for offset in range(ROUND))
CHUNKS = 4
ROWS = ROUND * CHIP // CHUNKS
LAST_IN_ORDER = ((((1,), (1,)), ((), ())))


def kernel(
    tok_hbm, gate_hbm, up_hbm, grad_hbm, routes_hbm, slots_hbm, mask_hbm,
    out_ref,
    tok, w, grad_t, routes, slots, mask, grad, sent, x_all, pre, g_all, ring, total, keep_own, keep, back,
    local_sem, x_send, x_recv, f_send, f_recv, b_send, b_recv, o_send, o_recv, k_send, k_recv,
):
    s, e, t = lax.axis_index("section"), lax.axis_index("expert"), lax.axis_index("tensor")
    chip, core = lax.div(e, 2), lax.rem(e, 2)
    width = tok.shape[1]
    half = gate_hbm.shape[0]

    def local(src, dst, index):
        copy = pltpu.make_async_copy(src, dst, local_sem.at[index])
        copy.start()
        return copy

    small = [
        local(routes_hbm, routes, 0), local(slots_hbm, slots, 1),
        local(mask_hbm, mask, 2), local(tok_hbm, tok, 3),
    ]
    large = [local(grad_hbm, grad_t, 4)]
    for rel in range(ROUND):
        columns = pl.ds(pl.multiple_of(lax.rem(t + rel, ROUND) * width, width), width)
        large.append(local(gate_hbm.at[:, columns], w.at[rel, pl.ds(0, half)], 5 + 2 * rel))
        large.append(local(up_hbm.at[:, columns], w.at[rel, pl.ds(half, half)], 6 + 2 * rel))

    up_z, down_z = lax.rem(t + 1, ROUND), lax.rem(t + ROUND - 1, ROUND)
    before, after = lax.rem(s + 7, 8), lax.rem(s + 1, 8)
    barrier = pltpu.get_barrier_semaphore()
    greeted = [(s, lax.rem(e + step, 16), t) for step in range(1, 16)]
    greeted += [(s, e, up_z), (s, e, down_z), (before, e, t), (after, e, t)]
    for device in greeted:
        pl.semaphore_signal(barrier, inc=1, device_id=device, device_id_type=MESH)

    for copy in small:
        copy.wait()
    live = (jnp.bitwise_and(routes[...], EXP_DEV - 1) == 0) & (slots[...] < CAP)
    target = jnp.where(live, lax.shift_right_logical(routes[...], 3) * CAP + slots[...], -1)
    positions = lax.broadcasted_iota(jnp.int32, (16 * CAP, tok.shape[0]), 0)
    hits = jnp.zeros(positions.shape, jnp.float32)
    for k in range(target.shape[0]):
        hits = hits + jnp.where(positions == target[k:k + 1, :], 1.0, 0.0)
    sent[...] = jnp.dot(
        hits.astype(jnp.bfloat16), tok[...], preferred_element_type=jnp.float32
    ).astype(jnp.bfloat16)
    x_all[0, pl.ds(pl.multiple_of(core * CAP, CAP), CAP)] = sent[pl.ds(pl.multiple_of(e * CAP, CAP), CAP)]

    pl.semaphore_wait(barrier, len(greeted))

    sends = []

    def ship(src, dst, send_sem, recv_sem, device):
        copy = pltpu.make_async_remote_copy(
            src_ref=src, dst_ref=dst, send_sem=send_sem, recv_sem=recv_sem,
            device_id=device, device_id_type=MESH,
        )
        copy.start()
        sends.append(copy)

    def to_expert(offset, other):
        to = lax.rem(chip + offset, ROUND) * 2 + other
        place = PLACE[(ROUND - offset) % ROUND]
        ship(
            sent.at[pl.ds(pl.multiple_of(to * CAP, CAP), CAP)],
            x_all.at[0, pl.ds(pl.multiple_of(place * CHIP + core * CAP, CAP), CAP)],
            x_send.at[PLACE[offset], other], x_recv.at[place, core], (s, to, t),
        )

    to_expert(0, 1 - core)
    for offset in NEAR[1:]:
        for other in range(2):
            to_expert(offset, other)

    keep_own[...] = jnp.transpose(hits * mask[...].astype(jnp.float32)).astype(jnp.bfloat16)
    ship(keep_own, keep, k_send.at[0], k_recv.at[0], (before, e, t))

    def landed(ref, send_sem, recv_sem):
        pltpu.make_async_remote_copy(
            src_ref=ref, dst_ref=ref, send_sem=send_sem, recv_sem=recv_sem,
            device_id=(s, e, up_z), device_id_type=MESH,
        ).wait_recv()

    def from_experts(place):
        for other in [1 - core] if place == 0 else range(2):
            rows = pl.ds(pl.multiple_of(place * CHIP + other * CAP, CAP), CAP)
            landed(x_all.at[0, rows], x_send.at[place, other], x_recv.at[place, other])

    def rows_of(chunk):
        return pl.ds(chunk * ROWS, ROWS)

    def up_steps(chunk):
        return 4 if chunk % 2 == 0 else 3

    def down_steps(chunk):
        return 7 - up_steps(chunk)

    def forward(chunk, step):
        rows = rows_of(chunk)
        if step < up_steps(chunk):
            ship(
                x_all.at[(ROUND - step) % ROUND, rows], x_all.at[ROUND - 1 - step, rows],
                f_send.at[0, chunk, step], f_recv.at[0, chunk, step], (s, e, up_z),
            )
        if step < down_steps(chunk):
            ship(
                x_all.at[step, rows], x_all.at[step + 1, rows],
                f_send.at[1, chunk, step], f_recv.at[1, chunk, step], (s, e, down_z),
            )

    def arrived(chunk, step):
        rows = rows_of(chunk)
        rels = []
        if step < up_steps(chunk):
            landed(x_all.at[ROUND - 1 - step, rows], f_send.at[0, chunk, step], f_recv.at[0, chunk, step])
            rels.append(ROUND - 1 - step)
        if step < down_steps(chunk):
            landed(x_all.at[step + 1, rows], f_send.at[1, chunk, step], f_recv.at[1, chunk, step])
            rels.append(step + 1)
        return rels

    def product(chunk, rel):
        return lax.dot_general(
            x_all[rel, chunk * ROWS:(chunk + 1) * ROWS], w[rel], LAST_IN_ORDER,
            preferred_element_type=jnp.float32,
        )

    for chunk in range(CHUNKS):
        for place in range(2 * chunk, 2 * chunk + 2):
            from_experts(place)
        forward(chunk, 0)
    for copy in large:
        copy.wait()
    grad[...] = jnp.transpose(grad_t[...].astype(jnp.float32))
    for chunk in range(CHUNKS):
        pre[chunk] = product(chunk, 0)

    def gradients(chunk):
        value = pre[chunk]
        gate, up = value[:, :half], value[:, half:]
        act = jnp.concatenate(
            [
                grad[pl.ds(pl.multiple_of(lax.rem(chip + NEAR[place], ROUND) * CHIP, CHIP), CHIP)]
                for place in range(2 * chunk, 2 * chunk + 2)
            ],
            axis=0,
        )
        sig = jax.nn.sigmoid(gate)
        up_grad = act * gate * sig
        gate_grad = act * up * sig * (1.0 + gate * (1.0 - sig))
        g_all[chunk] = jnp.concatenate([gate_grad, up_grad], axis=1).astype(jnp.bfloat16)

    def term(chunk, rel):
        return jnp.dot(g_all[chunk], w[rel % ROUND], preferred_element_type=jnp.float32)

    def add_and_send(chunk, direction, hops):
        steps = up_steps(chunk) if direction == 0 else down_steps(chunk)
        if hops > steps:
            return
        value = term(chunk, hops if direction == 0 else ROUND - hops)
        if hops < steps:
            landed(ring.at[direction, chunk, hops], b_send.at[direction, chunk, hops], b_recv.at[direction, chunk, hops])
            value = value + ring[direction, chunk, hops].astype(jnp.float32)
        ring[direction, chunk, hops] = value.astype(jnp.bfloat16)
        ship(
            ring.at[direction, chunk, hops], ring.at[direction, chunk, hops - 1],
            b_send.at[direction, chunk, hops - 1], b_recv.at[direction, chunk, hops - 1],
            (s, e, up_z if direction == 0 else down_z),
        )

    for step in range(4):
        for chunk in range(CHUNKS):
            rels = arrived(chunk, step)
            if step < 3:
                forward(chunk, step + 1)
            value = pre[chunk]
            for rel in rels:
                value = value + product(chunk, rel)
            pre[chunk] = value
            if step == 3:
                gradients(chunk)
                for hops in (4, 3):
                    for direction in range(2):
                        if hops == (up_steps(chunk), down_steps(chunk))[direction]:
                            add_and_send(chunk, direction, hops)

    order = (1, 2, 3, 0)
    for hops in (3, 2, 1):
        for chunk in order:
            for direction in range(2):
                if hops < (up_steps(chunk), down_steps(chunk))[direction]:
                    add_and_send(chunk, direction, hops)
    for chunk in order:
        value = term(chunk, 0)
        for direction in range(2):
            landed(ring.at[direction, chunk, 0], b_send.at[direction, chunk, 0], b_recv.at[direction, chunk, 0])
            value = value + ring[direction, chunk, 0].astype(jnp.float32)
        total[chunk] = value.astype(jnp.bfloat16)
        for place in range(2 * chunk, 2 * chunk + 2):
            for other in range(2):
                to = lax.rem(chip + NEAR[place], ROUND) * 2 + other
                ship(
                    total.at[chunk, pl.ds((place - 2 * chunk) * CHIP + other * CAP, CAP)],
                    back.at[pl.ds(pl.multiple_of(e * CAP, CAP), CAP)],
                    o_send.at[place, other], o_recv.at[e], (before, to, t),
                )

    landed(keep, k_send.at[0], k_recv.at[0])
    for source in range(16):
        landed(back.at[pl.ds(source * CAP, CAP)], o_send.at[0, 0], o_recv.at[source])
    result = jnp.dot(keep[...], back[...], preferred_element_type=jnp.float32)
    out_ref[...] = jnp.where(s == 7, 0.0, result).astype(out_ref.dtype)
    for copy in sends:
        copy.wait_send()


def shards(tokens, w_gate, w_up, hidden_grad, routes, slots, pad_mask):
    rows, width = tokens.shape
    features, half = w_gate.shape[2:]
    slot_rows = hidden_grad.shape[2]
    anywhere = pl.BlockSpec(memory_space=pl.ANY)
    dma = pltpu.SemaphoreType.DMA
    return pl.pallas_call(
        kernel,
        out_shape=jax.ShapeDtypeStruct(tokens.shape, tokens.dtype),
        in_specs=[anywhere] * 7,
        out_specs=pl.BlockSpec(memory_space=pltpu.VMEM),
        scratch_shapes=[
            pltpu.VMEM((rows, width), jnp.bfloat16),
            pltpu.VMEM((ROUND, 2 * half, width), jnp.bfloat16),
            pltpu.VMEM((half, slot_rows), jnp.bfloat16),
            pltpu.VMEM((routes.shape[1], rows), jnp.int32),
            pltpu.VMEM((routes.shape[1], rows), jnp.int32),
            pltpu.VMEM((1, rows), jnp.int32),
            pltpu.VMEM((slot_rows, half), jnp.float32),
            pltpu.VMEM((slot_rows, width), jnp.bfloat16),
            pltpu.VMEM((ROUND, slot_rows, width), jnp.bfloat16),
            pltpu.VMEM((CHUNKS, ROWS, 2 * half), jnp.float32),
            pltpu.VMEM((CHUNKS, ROWS, 2 * half), jnp.bfloat16),
            pltpu.VMEM((2, CHUNKS, 5, ROWS, width), jnp.bfloat16),
            pltpu.VMEM((CHUNKS, ROWS, width), jnp.bfloat16),
            pltpu.VMEM((rows, slot_rows), jnp.bfloat16),
            pltpu.VMEM((rows, slot_rows), jnp.bfloat16),
            pltpu.VMEM((slot_rows, width), jnp.bfloat16),
            dma((5 + 2 * ROUND,)),
            dma((ROUND, 2)),
            dma((ROUND, 2)),
            dma((2, CHUNKS, 4)),
            dma((2, CHUNKS, 4)),
            dma((2, CHUNKS, 4)),
            dma((2, CHUNKS, 4)),
            dma((ROUND, 2)),
            dma((16,)),
            dma((1,)),
            dma((1,)),
        ],
        compiler_params=pltpu.CompilerParams(
            collective_id=0, has_side_effects=True, vmem_limit_bytes=63 * 1024 * 1024
        ),
        cost_estimate=pl.CostEstimate(
            flops=8 * slot_rows * features * half, bytes_accessed=4 * features * half, transcendentals=0
        ),
    )(
        tokens, jnp.swapaxes(w_gate[0, 0], 0, 1), jnp.swapaxes(w_up[0, 0], 0, 1),
        jnp.swapaxes(hidden_grad[0, 0], 0, 1), jnp.swapaxes(routes, 0, 1), jnp.swapaxes(slots, 0, 1),
        pad_mask.reshape(1, rows),
    )


def solution(mesh):
    placed = (
        P(("section", "expert"), "tensor"),
        P("section", "expert", None, "tensor"),
        P("section", "expert", None, "tensor"),
        P("section", "expert", None, "tensor"),
        P(("section", "expert"), None),
        P(("section", "expert"), None),
        P(("section", "expert")),
    )
    return jax.shard_map(
        shards,
        mesh=mesh,
        in_specs=placed,
        out_specs=P(("section", "expert"), "tensor"),
        check_vma=False,
    )
```

```python
import jax
import jax.numpy as jnp
from jax import lax
from jax.experimental import pallas as pl
from jax.experimental.pallas import tpu as pltpu
from jax.sharding import PartitionSpec as P

MESH = pl.DeviceIdType.MESH
EXP_DEV = 8
CAP = 16
ROUND = 8
CHIP = 2 * CAP
NEAR = (0, 1, 7, 2, 6, 3, 5, 4)
PLACE = tuple(NEAR.index(offset) for offset in range(ROUND))
CHUNKS = 4
ORDER = (
    (0, 0, 1, 0), (0, 0, 0, 0), (0, 1, 1, 0), (0, 1, 0, 0), (0, 2, 0, 0), (0, 2, 1, 0), (1, 0, 0, 0), (0, 3, 1, 0),
    (1, 0, 1, 0), (0, 3, 0, 0), (1, 2, 1, 0), (1, 2, 0, 0), (1, 3, 1, 0), (1, 1, 1, 0), (1, 0, 0, 1), (1, 3, 0, 0),
    (1, 2, 1, 1), (1, 2, 0, 1), (1, 3, 1, 1), (1, 0, 0, 2), (1, 1, 0, 0), (1, 1, 1, 1), (1, 0, 1, 1), (1, 3, 0, 1),
    (1, 2, 1, 2), (1, 3, 1, 2), (1, 2, 0, 2), (1, 0, 0, 3), (1, 1, 1, 2), (1, 1, 0, 1), (1, 0, 1, 2), (2, 0, 0, 4),
    (2, 0, 1, 3), (1, 3, 0, 2), (1, 3, 1, 3), (2, 3, 0, 3), (2, 3, 1, 4), (1, 2, 0, 3), (2, 2, 1, 3), (2, 2, 0, 4),
    (1, 1, 1, 3), (1, 1, 0, 2), (2, 1, 1, 4), (2, 1, 0, 3), (2, 3, 1, 3), (2, 0, 1, 2), (2, 3, 0, 2), (2, 2, 0, 3),
    (2, 1, 1, 3), (2, 1, 0, 2), (2, 3, 1, 2), (2, 2, 1, 2), (2, 0, 0, 3), (2, 2, 0, 2), (2, 1, 1, 2), (2, 3, 0, 1),
    (2, 3, 1, 1), (2, 0, 0, 2), (2, 2, 1, 1), (2, 2, 0, 1), (2, 1, 0, 1), (2, 1, 1, 1), (3, 3, 0, 0), (2, 0, 0, 1),
    (2, 0, 1, 1), (3, 2, 0, 0), (3, 1, 0, 0), (3, 0, 0, 0),
)
PER = ROUND // CHUNKS
ROWS = PER * CHIP
LAST_IN_ORDER = ((((1,), (1,)), ((), ())))


def kernel(
    tok_hbm, gate_hbm, up_hbm, grad_hbm, routes_hbm, slots_hbm, mask_hbm,
    out_ref,
    tok, w, grad_t, routes, slots, mask, grad, sent, x_all, pre, g_all, ring, total, keep_own, keep, back,
    local_sem, x_send, x_recv, f_send, f_recv, b_send, b_recv, o_send, o_recv, k_send, k_recv, ready,
):
    s, e, t = lax.axis_index("section"), lax.axis_index("expert"), lax.axis_index("tensor")
    chip, core = lax.div(e, 2), lax.rem(e, 2)
    width = tok.shape[1]
    half = gate_hbm.shape[0]

    def local(src, dst, index):
        copy = pltpu.make_async_copy(src, dst, local_sem.at[index])
        copy.start()
        return copy

    small = [
        local(routes_hbm, routes, 0), local(slots_hbm, slots, 1),
        local(mask_hbm, mask, 2), local(tok_hbm, tok, 3),
    ]
    large = [local(grad_hbm, grad_t, 4)]
    for rel in range(ROUND):
        columns = pl.ds(pl.multiple_of(lax.rem(t + rel, ROUND) * width, width), width)
        large.append(local(gate_hbm.at[:, columns], w.at[rel, pl.ds(0, half)], 5 + 2 * rel))
        large.append(local(up_hbm.at[:, columns], w.at[rel, pl.ds(half, half)], 6 + 2 * rel))

    up_z, down_z = lax.rem(t + 1, ROUND), lax.rem(t + ROUND - 1, ROUND)
    before, after = lax.rem(s + 7, 8), lax.rem(s + 1, 8)
    barrier = pltpu.get_barrier_semaphore()
    greeted = [(s, lax.rem(e + step, 16), t) for step in range(1, 16)]
    greeted += [(before, e, t), (after, e, t)]
    for device in greeted:
        pl.semaphore_signal(barrier, inc=1, device_id=device, device_id_type=MESH)

    @pl.when(t < ROUND - 1)
    def _():
        pl.semaphore_signal(barrier, inc=1, device_id=(s, e, up_z), device_id_type=MESH)

    @pl.when(t == 0)
    def _():
        pl.semaphore_signal(barrier, inc=1, device_id=(s, e, down_z), device_id_type=MESH)

    for copy in small:
        copy.wait()
    live = (jnp.bitwise_and(routes[...], EXP_DEV - 1) == 0) & (slots[...] < CAP)
    target = jnp.where(live, lax.shift_right_logical(routes[...], 3) * CAP + slots[...], -1)
    positions = lax.broadcasted_iota(jnp.int32, (16 * CAP, tok.shape[0]), 0)
    hits = jnp.zeros(positions.shape, jnp.float32)
    for k in range(target.shape[0]):
        hits = hits + jnp.where(positions == target[k:k + 1, :], 1.0, 0.0)
    sent[...] = jnp.dot(
        hits.astype(jnp.bfloat16), tok[...], preferred_element_type=jnp.float32
    ).astype(jnp.bfloat16)
    x_all[0, pl.ds(pl.multiple_of(core * CAP, CAP), CAP)] = sent[pl.ds(pl.multiple_of(e * CAP, CAP), CAP)]

    pl.semaphore_wait(barrier, len(greeted) + (t + ROUND - 1) // ROUND + t // (ROUND - 1))

    @pl.when(t > 0)
    def _():
        pl.semaphore_signal(ready.at[0], inc=1, device_id=(s, e, down_z), device_id_type=MESH)

    @pl.when(t == ROUND - 1)
    def _():
        pl.semaphore_signal(ready.at[1], inc=1, device_id=(s, e, up_z), device_id_type=MESH)

    sends = {}

    def ship(operands, *name):
        def copy():
            src, dst, send_sem, recv_sem, device = operands()
            return pltpu.make_async_remote_copy(
                src_ref=src, dst_ref=dst, send_sem=send_sem, recv_sem=recv_sem,
                device_id=device, device_id_type=MESH,
            )

        copy().start()
        sends[name] = copy

    def to_expert(offset, other):
        to = lax.rem(chip + offset, ROUND) * 2 + other
        place = PLACE[(ROUND - offset) % ROUND]
        ship(lambda: (
            sent.at[pl.ds(pl.multiple_of(to * CAP, CAP), CAP)],
            x_all.at[0, pl.ds(pl.multiple_of(place * CHIP + core * CAP, CAP), CAP)],
            x_send.at[PLACE[offset], other], x_recv.at[place, core], (s, to, t)
        ), "x", offset, 0 if offset == 0 else other)

    to_expert(0, 1 - core)
    for offset in NEAR[1:]:
        for other in range(2):
            to_expert(offset, other)

    keep_own[...] = jnp.transpose(hits * mask[...].astype(jnp.float32)).astype(jnp.bfloat16)
    ship(lambda: (keep_own, keep, k_send.at[0], k_recv.at[0], (before, e, t)), "k")

    def landed(ref, send_sem, recv_sem):
        pltpu.make_async_remote_copy(
            src_ref=ref, dst_ref=ref, send_sem=send_sem, recv_sem=recv_sem,
            device_id=(s, e, up_z), device_id_type=MESH,
        ).wait_recv()

    def from_experts(place):
        for other in [1 - core] if place == 0 else range(2):
            rows = pl.ds(pl.multiple_of(place * CHIP + other * CAP, CAP), CAP)
            landed(x_all.at[0, rows], x_send.at[place, other], x_recv.at[place, other])

    def places(chunk):
        return range(PER * chunk, PER * (chunk + 1))

    def rows_of(chunk):
        return pl.ds(chunk * ROWS, ROWS)

    def up_steps(chunk):
        return 4 if chunk % 2 == 0 else 3

    def down_steps(chunk):
        return 7 - up_steps(chunk)

    def forward(chunk, step, directions=(0, 1)):
        rows = rows_of(chunk)
        if step < up_steps(chunk) and 0 in directions:
            ship(lambda: (
                x_all.at[(ROUND - step) % ROUND, rows], x_all.at[ROUND - 1 - step, rows],
                f_send.at[0, chunk, step], f_recv.at[0, chunk, step], (s, e, up_z)
            ), "f", 0, chunk, step)
        if step < down_steps(chunk) and 1 in directions:
            ship(lambda: (
                x_all.at[step, rows], x_all.at[step + 1, rows],
                f_send.at[1, chunk, step], f_recv.at[1, chunk, step], (s, e, down_z)
            ), "f", 1, chunk, step)

    def arrived(chunk, step, directions=(0, 1)):
        rows = rows_of(chunk)
        rels = []
        if step < up_steps(chunk) and 0 in directions:
            landed(x_all.at[ROUND - 1 - step, rows], f_send.at[0, chunk, step], f_recv.at[0, chunk, step])
            rels.append(ROUND - 1 - step)
        if step < down_steps(chunk) and 1 in directions:
            landed(x_all.at[step + 1, rows], f_send.at[1, chunk, step], f_recv.at[1, chunk, step])
            rels.append(step + 1)
        return rels

    def product(chunk, rel):
        return lax.dot_general(
            x_all[rel, chunk * ROWS:(chunk + 1) * ROWS], w[rel], LAST_IN_ORDER,
            preferred_element_type=jnp.float32,
        )

    def gradients(chunk):
        value = pre[chunk]
        gate, up = value[:, :half], value[:, half:]
        act = jnp.concatenate(
            [
                grad[pl.ds(pl.multiple_of(lax.rem(chip + NEAR[place], ROUND) * CHIP, CHIP), CHIP)]
                for place in places(chunk)
            ],
            axis=0,
        )
        sig = jax.nn.sigmoid(gate)
        up_grad = act * gate * sig
        gate_grad = act * up * sig * (1.0 + gate * (1.0 - sig))
        g_all[chunk] = jnp.concatenate([gate_grad, up_grad], axis=1).astype(jnp.bfloat16)

    def term(chunk, rel):
        return jnp.dot(g_all[chunk], w[rel % ROUND], preferred_element_type=jnp.float32)

    def add_and_send(chunk, direction, hops):
        steps = up_steps(chunk) if direction == 0 else down_steps(chunk)
        if hops > steps:
            return
        value = term(chunk, hops if direction == 0 else ROUND - hops)
        if hops < steps:
            landed(ring.at[direction, chunk, hops], b_send.at[direction, chunk, hops], b_recv.at[direction, chunk, hops])
            value = value + ring[direction, chunk, hops].astype(jnp.float32)
        ring[direction, chunk, hops] = value.astype(jnp.bfloat16)
        ship(lambda: (
            ring.at[direction, chunk, hops], ring.at[direction, chunk, hops - 1],
            b_send.at[direction, chunk, hops - 1], b_recv.at[direction, chunk, hops - 1],
            (s, e, up_z if direction == 0 else down_z)
        ), "b", direction, chunk, hops)

    def to_tokens(place, other):
        to = lax.rem(chip + NEAR[place], ROUND) * 2 + other
        ship(lambda: (
            total.at[place // PER, pl.ds(place % PER * CHIP + other * CAP, CAP)],
            back.at[pl.ds(pl.multiple_of(e * CAP, CAP), CAP)],
            o_send.at[place, other], o_recv.at[e], (before, to, t)
        ), "o", place, other)

    def own(chunk, direction, _):
        if chunk not in begun:
            for place in places(chunk):
                from_experts(place)
            begun.add(chunk)
        if direction not in met:
            met.add(direction)

            @pl.when(t < ROUND - 1 if direction == 0 else t == 0)
            def _():
                pl.semaphore_wait(ready.at[direction], 1)

        forward(chunk, 0, (direction,))
        if direction == 0:
            take(chunk, 0)

    def pass_on(chunk, direction, step):
        (rel,) = arrived(chunk, step, (direction,))
        forward(chunk, step + 1, (direction,))
        take(chunk, rel)

    def take(chunk, rel):
        if not filled:
            for copy in large:
                copy.wait()
            grad[...] = jnp.transpose(grad_t[...].astype(jnp.float32))
        if chunk in filled:
            pre[chunk] += product(chunk, rel)
        else:
            pre[chunk] = product(chunk, rel)
        filled.add(chunk)

    def add(chunk, direction, hops):
        if chunk not in turned:
            gradients(chunk)
            turned.add(chunk)
        add_and_send(chunk, direction, hops)

    def finish(chunk, *_):
        value = term(chunk, 0)
        for direction in range(2):
            landed(ring.at[direction, chunk, 0], b_send.at[direction, chunk, 0], b_recv.at[direction, chunk, 0])
            value = value + ring[direction, chunk, 0].astype(jnp.float32)
        total[chunk] = value.astype(jnp.bfloat16)
        for place in places(chunk):
            for other in range(2):
                to_tokens(place, other)

    begun, met, filled, turned = set(), set(), set(), set()
    for kind, chunk, direction, step in ORDER:
        (own, pass_on, add, finish)[kind](chunk, direction, step)

    landed(keep, k_send.at[0], k_recv.at[0])
    for source in range(16):
        landed(back.at[pl.ds(source * CAP, CAP)], o_send.at[0, 0], o_recv.at[source])
    result = jnp.dot(keep[...], back[...], preferred_element_type=jnp.float32)
    out_ref[...] = jnp.where(s == 7, 0.0, result).astype(out_ref.dtype)
    for copy in sends.values():
        copy().wait_send()


def shards(tokens, w_gate, w_up, hidden_grad, routes, slots, pad_mask):
    rows, width = tokens.shape
    features, half = w_gate.shape[2:]
    slot_rows = hidden_grad.shape[2]
    anywhere = pl.BlockSpec(memory_space=pl.ANY)
    dma = pltpu.SemaphoreType.DMA
    return pl.pallas_call(
        kernel,
        out_shape=jax.ShapeDtypeStruct(tokens.shape, tokens.dtype),
        in_specs=[anywhere] * 7,
        out_specs=pl.BlockSpec(memory_space=pltpu.VMEM),
        scratch_shapes=[
            pltpu.VMEM((rows, width), jnp.bfloat16),
            pltpu.VMEM((ROUND, 2 * half, width), jnp.bfloat16),
            pltpu.VMEM((half, slot_rows), jnp.bfloat16),
            pltpu.VMEM((routes.shape[1], rows), jnp.int32),
            pltpu.VMEM((routes.shape[1], rows), jnp.int32),
            pltpu.VMEM((1, rows), jnp.int32),
            pltpu.VMEM((slot_rows, half), jnp.float32),
            pltpu.VMEM((slot_rows, width), jnp.bfloat16),
            pltpu.VMEM((ROUND, slot_rows, width), jnp.bfloat16),
            pltpu.VMEM((CHUNKS, ROWS, 2 * half), jnp.float32),
            pltpu.VMEM((CHUNKS, ROWS, 2 * half), jnp.bfloat16),
            pltpu.VMEM((2, CHUNKS, 5, ROWS, width), jnp.bfloat16),
            pltpu.VMEM((CHUNKS, ROWS, width), jnp.bfloat16),
            pltpu.VMEM((rows, slot_rows), jnp.bfloat16),
            pltpu.VMEM((rows, slot_rows), jnp.bfloat16),
            pltpu.VMEM((slot_rows, width), jnp.bfloat16),
            dma((5 + 2 * ROUND,)),
            dma((ROUND, 2)),
            dma((ROUND, 2)),
            dma((2, CHUNKS, 4)),
            dma((2, CHUNKS, 4)),
            dma((2, CHUNKS, 4)),
            dma((2, CHUNKS, 4)),
            dma((ROUND, 2)),
            dma((16,)),
            dma((1,)),
            dma((1,)),
            pltpu.SemaphoreType.REGULAR((2,)),
        ],
        compiler_params=pltpu.CompilerParams(
            collective_id=0, has_side_effects=True, vmem_limit_bytes=63 * 1024 * 1024
        ),
        cost_estimate=pl.CostEstimate(
            flops=8 * slot_rows * features * half, bytes_accessed=4 * features * half, transcendentals=0
        ),
    )(
        tokens, jnp.swapaxes(w_gate[0, 0], 0, 1), jnp.swapaxes(w_up[0, 0], 0, 1),
        jnp.swapaxes(hidden_grad[0, 0], 0, 1), jnp.swapaxes(routes, 0, 1), jnp.swapaxes(slots, 0, 1),
        pad_mask.reshape(1, rows),
    )


def solution(mesh):
    placed = (
        P(("section", "expert"), "tensor"),
        P("section", "expert", None, "tensor"),
        P("section", "expert", None, "tensor"),
        P("section", "expert", None, "tensor"),
        P(("section", "expert"), None),
        P(("section", "expert"), None),
        P(("section", "expert")),
    )
    return jax.shard_map(
        shards,
        mesh=mesh,
        in_specs=placed,
        out_specs=P(("section", "expert"), "tensor"),
        check_vma=False,
    )
```

```python
import jax
import jax.numpy as jnp
from jax import lax
from jax.experimental import pallas as pl
from jax.experimental.pallas import tpu as pltpu
from jax.sharding import PartitionSpec as P

MESH = pl.DeviceIdType.MESH
EXP_DEV = 8
CAP = 16
ROUND = 8
CHIP = 2 * CAP
NEAR = (0, 1, 7, 2, 6, 3, 5, 4)
PLACE = tuple(NEAR.index(offset) for offset in range(ROUND))
CHUNKS = 4
ORDER = (
    (0, 0, 1, 0), (0, 0, 0, 0), (0, 1, 1, 0), (0, 1, 0, 0), (0, 2, 0, 0), (0, 2, 1, 0), (1, 0, 0, 0), (0, 3, 1, 0),
    (1, 0, 1, 0), (0, 3, 0, 0), (1, 2, 1, 0), (1, 2, 0, 0), (1, 3, 1, 0), (1, 1, 1, 0), (1, 0, 0, 1), (1, 3, 0, 0),
    (1, 2, 1, 1), (1, 2, 0, 1), (1, 3, 1, 1), (1, 0, 0, 2), (1, 1, 0, 0), (1, 1, 1, 1), (1, 0, 1, 1), (1, 3, 0, 1),
    (1, 2, 1, 2), (1, 3, 1, 2), (1, 2, 0, 2), (1, 0, 0, 3), (1, 1, 1, 2), (1, 1, 0, 1), (1, 0, 1, 2), (2, 0, 0, 4),
    (2, 0, 1, 3), (1, 3, 0, 2), (1, 3, 1, 3), (2, 3, 0, 3), (2, 3, 1, 4), (1, 2, 0, 3), (2, 2, 1, 3), (2, 2, 0, 4),
    (1, 1, 1, 3), (1, 1, 0, 2), (2, 1, 1, 4), (2, 1, 0, 3), (2, 3, 1, 3), (2, 0, 1, 2), (2, 3, 0, 2), (2, 2, 0, 3),
    (2, 1, 1, 3), (2, 1, 0, 2), (2, 3, 1, 2), (2, 2, 1, 2), (2, 0, 0, 3), (2, 2, 0, 2), (2, 1, 1, 2), (2, 3, 0, 1),
    (2, 3, 1, 1), (2, 0, 0, 2), (2, 2, 1, 1), (2, 2, 0, 1), (2, 1, 0, 1), (2, 1, 1, 1), (3, 3, 0, 0), (2, 0, 0, 1),
    (2, 0, 1, 1), (3, 2, 0, 0), (3, 1, 0, 0), (3, 0, 0, 0),
)
IN_FLIGHT = 3
PER = ROUND // CHUNKS
ROWS = PER * CHIP
LAST_IN_ORDER = ((((1,), (1,)), ((), ())))


def kernel(
    tok_hbm, gate_hbm, up_hbm, grad_hbm, routes_hbm, slots_hbm, mask_hbm,
    keep, back,
    tok, w, grad_t, routes, slots, mask, grad, sent, x_all, pre, g_all, ring, total, keep_own,
    local_sem, x_send, x_recv, f_send, f_recv, b_send, b_recv, o_send, o_recv, k_send, k_recv, ready,
):
    s, e, t = lax.axis_index("section"), lax.axis_index("expert"), lax.axis_index("tensor")
    chip, core = lax.div(e, 2), lax.rem(e, 2)
    width = tok.shape[1]
    half = gate_hbm.shape[0]

    def local(src, dst, index):
        copy = pltpu.make_async_copy(src, dst, local_sem.at[index])
        copy.start()
        return copy

    small = [
        local(routes_hbm, routes, 0), local(slots_hbm, slots, 1),
        local(mask_hbm, mask, 2), local(tok_hbm, tok, 3),
    ]
    large = [local(grad_hbm, grad_t, 4)]
    for rel in range(ROUND):
        columns = pl.ds(pl.multiple_of(lax.rem(t + rel, ROUND) * width, width), width)
        large.append(local(gate_hbm.at[:, columns], w.at[rel, pl.ds(0, half)], 5 + 2 * rel))
        large.append(local(up_hbm.at[:, columns], w.at[rel, pl.ds(half, half)], 6 + 2 * rel))

    up_z, down_z = lax.rem(t + 1, ROUND), lax.rem(t + ROUND - 1, ROUND)
    before, after = lax.rem(s + 7, 8), lax.rem(s + 1, 8)
    barrier = pltpu.get_barrier_semaphore()
    greeted = [(s, lax.rem(e + step, 16), t) for step in range(1, 16)]
    greeted += [(before, e, t), (after, e, t)]
    for device in greeted:
        pl.semaphore_signal(barrier, inc=1, device_id=device, device_id_type=MESH)

    @pl.when(t < ROUND - 1)
    def _():
        pl.semaphore_signal(barrier, inc=1, device_id=(s, e, up_z), device_id_type=MESH)

    @pl.when(t == 0)
    def _():
        pl.semaphore_signal(barrier, inc=1, device_id=(s, e, down_z), device_id_type=MESH)

    for copy in small:
        copy.wait()
    live = (jnp.bitwise_and(routes[...], EXP_DEV - 1) == 0) & (slots[...] < CAP)
    target = jnp.where(live, lax.shift_right_logical(routes[...], 3) * CAP + slots[...], -1)
    positions = lax.broadcasted_iota(jnp.int32, (16 * CAP, tok.shape[0]), 0)
    hits = jnp.zeros(positions.shape, jnp.float32)
    for k in range(target.shape[0]):
        hits = hits + jnp.where(positions == target[k:k + 1, :], 1.0, 0.0)
    sent[...] = jnp.dot(
        hits.astype(jnp.bfloat16), tok[...], preferred_element_type=jnp.float32
    ).astype(jnp.bfloat16)
    x_all[0, pl.ds(pl.multiple_of(core * CAP, CAP), CAP)] = sent[pl.ds(pl.multiple_of(e * CAP, CAP), CAP)]

    pl.semaphore_wait(barrier, len(greeted) + (t + ROUND - 1) // ROUND + t // (ROUND - 1))

    @pl.when(t > 0)
    def _():
        pl.semaphore_signal(ready.at[0], inc=1, device_id=(s, e, down_z), device_id_type=MESH)

    @pl.when(t == ROUND - 1)
    def _():
        pl.semaphore_signal(ready.at[1], inc=1, device_id=(s, e, up_z), device_id_type=MESH)

    sends, queues = {}, ([], [])

    def ship(operands, *name):
        def copy():
            src, dst, send_sem, recv_sem, device = operands()
            return pltpu.make_async_remote_copy(
                src_ref=src, dst_ref=dst, send_sem=send_sem, recv_sem=recv_sem,
                device_id=device, device_id_type=MESH,
            )

        if name[0] in ("f", "b"):
            queue = queues[name[1]]
            queue.append(name)
            if len(queue) > IN_FLIGHT:
                sends.pop(queue.pop(0))().wait_send()
        copy().start()
        sends[name] = copy

    def to_expert(offset, other):
        to = lax.rem(chip + offset, ROUND) * 2 + other
        place = PLACE[(ROUND - offset) % ROUND]
        ship(lambda: (
            sent.at[pl.ds(pl.multiple_of(to * CAP, CAP), CAP)],
            x_all.at[0, pl.ds(pl.multiple_of(place * CHIP + core * CAP, CAP), CAP)],
            x_send.at[PLACE[offset], other], x_recv.at[place, core], (s, to, t)
        ), "x", offset, 0 if offset == 0 else other)

    to_expert(0, 1 - core)
    for offset in NEAR[1:]:
        for other in range(2):
            to_expert(offset, other)

    keep_own[...] = jnp.transpose(hits * mask[...].astype(jnp.float32)).astype(jnp.bfloat16)
    ship(lambda: (keep_own, keep, k_send.at[0], k_recv.at[0], (before, e, t)), "k")

    def landed(ref, send_sem, recv_sem):
        pltpu.make_async_remote_copy(
            src_ref=ref, dst_ref=ref, send_sem=send_sem, recv_sem=recv_sem,
            device_id=(s, e, up_z), device_id_type=MESH,
        ).wait_recv()

    def from_experts(place):
        for other in [1 - core] if place == 0 else range(2):
            rows = pl.ds(pl.multiple_of(place * CHIP + other * CAP, CAP), CAP)
            landed(x_all.at[0, rows], x_send.at[place, other], x_recv.at[place, other])

    def places(chunk):
        return range(PER * chunk, PER * (chunk + 1))

    def rows_of(chunk):
        return pl.ds(chunk * ROWS, ROWS)

    def up_steps(chunk):
        return 4 if chunk % 2 == 0 else 3

    def down_steps(chunk):
        return 7 - up_steps(chunk)

    def forward(chunk, step, directions=(0, 1)):
        rows = rows_of(chunk)
        if step < up_steps(chunk) and 0 in directions:
            ship(lambda: (
                x_all.at[(ROUND - step) % ROUND, rows], x_all.at[ROUND - 1 - step, rows],
                f_send.at[0, chunk, step], f_recv.at[0, chunk, step], (s, e, up_z)
            ), "f", 0, chunk, step)
        if step < down_steps(chunk) and 1 in directions:
            ship(lambda: (
                x_all.at[step, rows], x_all.at[step + 1, rows],
                f_send.at[1, chunk, step], f_recv.at[1, chunk, step], (s, e, down_z)
            ), "f", 1, chunk, step)

    def arrived(chunk, step, directions=(0, 1)):
        rows = rows_of(chunk)
        rels = []
        if step < up_steps(chunk) and 0 in directions:
            landed(x_all.at[ROUND - 1 - step, rows], f_send.at[0, chunk, step], f_recv.at[0, chunk, step])
            rels.append(ROUND - 1 - step)
        if step < down_steps(chunk) and 1 in directions:
            landed(x_all.at[step + 1, rows], f_send.at[1, chunk, step], f_recv.at[1, chunk, step])
            rels.append(step + 1)
        return rels

    def product(chunk, rel):
        return lax.dot_general(
            x_all[rel, chunk * ROWS:(chunk + 1) * ROWS], w[rel], LAST_IN_ORDER,
            preferred_element_type=jnp.float32,
        )

    def gradients(chunk):
        value = pre[chunk]
        gate, up = value[:, :half], value[:, half:]
        act = jnp.concatenate(
            [
                grad[pl.ds(pl.multiple_of(lax.rem(chip + NEAR[place], ROUND) * CHIP, CHIP), CHIP)]
                for place in places(chunk)
            ],
            axis=0,
        )
        sig = jax.nn.sigmoid(gate)
        up_grad = act * gate * sig
        gate_grad = act * up * sig * (1.0 + gate * (1.0 - sig))
        g_all[chunk] = jnp.concatenate([gate_grad, up_grad], axis=1).astype(jnp.bfloat16)

    def term(chunk, rel):
        return jnp.dot(g_all[chunk], w[rel % ROUND], preferred_element_type=jnp.float32)

    def add_and_send(chunk, direction, hops):
        steps = up_steps(chunk) if direction == 0 else down_steps(chunk)
        if hops > steps:
            return
        value = term(chunk, hops if direction == 0 else ROUND - hops)
        if hops < steps:
            landed(ring.at[direction, chunk, hops], b_send.at[direction, chunk, hops], b_recv.at[direction, chunk, hops])
            value = value + ring[direction, chunk, hops].astype(jnp.float32)
        ring[direction, chunk, hops] = value.astype(jnp.bfloat16)
        ship(lambda: (
            ring.at[direction, chunk, hops], ring.at[direction, chunk, hops - 1],
            b_send.at[direction, chunk, hops - 1], b_recv.at[direction, chunk, hops - 1],
            (s, e, up_z if direction == 0 else down_z)
        ), "b", direction, chunk, hops)

    def to_tokens(place, other):
        to = lax.rem(chip + NEAR[place], ROUND) * 2 + other
        ship(lambda: (
            total.at[place // PER, pl.ds(place % PER * CHIP + other * CAP, CAP)],
            back.at[pl.ds(pl.multiple_of(e * CAP, CAP), CAP)],
            o_send.at[place, other], o_recv.at[e], (before, to, t)
        ), "o", place, other)

    def own(chunk, direction, _):
        if chunk not in begun:
            for place in places(chunk):
                from_experts(place)
            begun.add(chunk)
        if direction not in met:
            met.add(direction)

            @pl.when(t < ROUND - 1 if direction == 0 else t == 0)
            def _():
                pl.semaphore_wait(ready.at[direction], 1)

        forward(chunk, 0, (direction,))
        if direction == 0:
            take(chunk, 0)

    def pass_on(chunk, direction, step):
        (rel,) = arrived(chunk, step, (direction,))
        forward(chunk, step + 1, (direction,))
        take(chunk, rel)

    def take(chunk, rel):
        if not filled:
            for copy in large:
                copy.wait()
            grad[...] = jnp.transpose(grad_t[...].astype(jnp.float32))
        if chunk in filled:
            pre[chunk] += product(chunk, rel)
        else:
            pre[chunk] = product(chunk, rel)
        filled.add(chunk)

    def add(chunk, direction, hops):
        if chunk not in turned:
            gradients(chunk)
            turned.add(chunk)
        add_and_send(chunk, direction, hops)

    def finish(chunk, *_):
        value = term(chunk, 0)
        for direction in range(2):
            landed(ring.at[direction, chunk, 0], b_send.at[direction, chunk, 0], b_recv.at[direction, chunk, 0])
            value = value + ring[direction, chunk, 0].astype(jnp.float32)
        total[chunk] = value.astype(jnp.bfloat16)
        for place in places(chunk):
            for other in range(2):
                to_tokens(place, other)

    begun, met, filled, turned = set(), set(), set(), set()
    for kind, chunk, direction, step in ORDER:
        (own, pass_on, add, finish)[kind](chunk, direction, step)

    last = [copy for name, copy in sends.items() if name[0] == "o"]
    for name, copy in sends.items():
        if name[0] != "o":
            copy().wait_send()
    landed(keep, k_send.at[0], k_recv.at[0])
    for source in range(16):
        landed(back.at[pl.ds(source * CAP, CAP)], o_send.at[0, 0], o_recv.at[source])
    for copy in last:
        copy().wait_send()


def shards(tokens, w_gate, w_up, hidden_grad, routes, slots, pad_mask):
    rows, width = tokens.shape
    features, half = w_gate.shape[2:]
    slot_rows = hidden_grad.shape[2]
    anywhere = pl.BlockSpec(memory_space=pl.ANY)
    dma = pltpu.SemaphoreType.DMA
    keep, back = pl.pallas_call(
        kernel,
        out_shape=[
            jax.ShapeDtypeStruct((rows, slot_rows), jnp.bfloat16),
            jax.ShapeDtypeStruct((slot_rows, width), jnp.bfloat16),
        ],
        in_specs=[anywhere] * 7,
        out_specs=[anywhere] * 2,
        scratch_shapes=[
            pltpu.VMEM((rows, width), jnp.bfloat16),
            pltpu.VMEM((ROUND, 2 * half, width), jnp.bfloat16),
            pltpu.VMEM((half, slot_rows), jnp.bfloat16),
            pltpu.VMEM((routes.shape[1], rows), jnp.int32),
            pltpu.VMEM((routes.shape[1], rows), jnp.int32),
            pltpu.VMEM((1, rows), jnp.int32),
            pltpu.VMEM((slot_rows, half), jnp.float32),
            pltpu.VMEM((slot_rows, width), jnp.bfloat16),
            pltpu.VMEM((ROUND, slot_rows, width), jnp.bfloat16),
            pltpu.VMEM((CHUNKS, ROWS, 2 * half), jnp.float32),
            pltpu.VMEM((CHUNKS, ROWS, 2 * half), jnp.bfloat16),
            pltpu.VMEM((2, CHUNKS, 5, ROWS, width), jnp.bfloat16),
            pltpu.VMEM((CHUNKS, ROWS, width), jnp.bfloat16),
            pltpu.VMEM((rows, slot_rows), jnp.bfloat16),
            dma((5 + 2 * ROUND,)),
            dma((ROUND, 2)),
            dma((ROUND, 2)),
            dma((2, CHUNKS, 4)),
            dma((2, CHUNKS, 4)),
            dma((2, CHUNKS, 4)),
            dma((2, CHUNKS, 4)),
            dma((ROUND, 2)),
            dma((16,)),
            dma((1,)),
            dma((1,)),
            pltpu.SemaphoreType.REGULAR((2,)),
        ],
        compiler_params=pltpu.CompilerParams(
            collective_id=0, has_side_effects=True, vmem_limit_bytes=63 * 1024 * 1024
        ),
        cost_estimate=pl.CostEstimate(
            flops=8 * slot_rows * features * half, bytes_accessed=4 * features * half, transcendentals=0
        ),
    )(
        tokens, jnp.swapaxes(w_gate[0, 0], 0, 1), jnp.swapaxes(w_up[0, 0], 0, 1),
        jnp.swapaxes(hidden_grad[0, 0], 0, 1), jnp.swapaxes(routes, 0, 1), jnp.swapaxes(slots, 0, 1),
        pad_mask.reshape(1, rows),
    )
    result = jnp.dot(keep, back, preferred_element_type=jnp.float32)
    return jnp.where(lax.axis_index("section") == 7, 0.0, result).astype(tokens.dtype)


def solution(mesh):
    placed = (
        P(("section", "expert"), "tensor"),
        P("section", "expert", None, "tensor"),
        P("section", "expert", None, "tensor"),
        P("section", "expert", None, "tensor"),
        P(("section", "expert"), None),
        P(("section", "expert"), None),
        P(("section", "expert")),
    )
    return jax.shard_map(
        shards,
        mesh=mesh,
        in_specs=placed,
        out_specs=P(("section", "expert"), "tensor"),
        check_vma=False,
    )
```
